32 devices in a mesh: grp: 4 (over y, core), orb: 8 (over z, x).
Axes of the slice: x: 2, y: 2, z: 4, core: 2. Of those that a mesh axis runs over, the one named last changes fastest.
Arguments:
- slabs: float32 [32, 256, 1024], P(('grp', 'orb')), may hold values from -0.9 to 0.9
- eps_occ: float32 [32], P(('grp', 'orb')), may hold values from -1.5 to -0.5
- eps_vir: float32 [256], replicated, may hold values from 0.2 to 3
Outputs:
- gradient: float32 [32, 256, 1024], P(('grp', 'orb'))
- density: float32 [256, 256], P('orb')
The draws below stay inside these ranges and needn't reach their ends.
All inputs are finite; a program needn't handle non-finite values.
Results may differ from the reference program's by a relative error of at most 0.0003.
Values sent between devices are 32-bit elements; how exact they have to be, the bound alone decides.
A program may use at most 64 MiB of HBM per device.

```python
import jax
import jax.numpy as jnp
from jax import lax

V = 256
NAUX = 1024
NOCC = 32


def levels(rng, extent, pieces, smallest, largest):
    factor_of, own = 1.0, jax.random.fold_in(rng, 6)
    for axis_at, shards_of in pieces:
        heights = jnp.exp(jax.random.uniform(jax.random.fold_in(own, axis_at), (shards_of,), jnp.float32, smallest / len(pieces), largest / len(pieces)))
        factor_of = factor_of * jnp.repeat(heights, extent[axis_at] // shards_of).reshape([-1 if axis == axis_at else 1 for axis in range(len(extent))])
    return factor_of


def scatter_about(rng, shape, spread, limit, cuts=(), kind=jnp.bfloat16):
    result = spread * jax.random.normal(rng, shape, jnp.float32)
    if cuts:
        result = result * levels(rng, shape, cuts, -0.22, 0.18)
    return jnp.clip(result, -limit, limit).astype(kind)


def setup_inputs(seed: int = 0) -> dict:
    key_list = jax.random.split(jax.random.key(seed), 4)
    slabs = scatter_about(key_list[0], (NOCC, V, NAUX), 0.15, 0.9, ((0, 32),), jnp.float32)
    eps_occ = jnp.clip(-1.5 + 1.0 * jax.random.uniform(key_list[1], (NOCC,), jnp.float32) ** levels(key_list[1], (NOCC,), ((0, 32),), -0.2, 0.2), -1.5, -0.5)
    eps_vir = jnp.clip(jax.random.uniform(key_list[2], (V,), jnp.float32, 0.2, 3.0), 0.2, 3.0)
    return {"slabs": slabs, "eps_occ": eps_occ, "eps_vir": eps_vir}


def pair_terms(own, other, e_own, e_other, eps_vir):
    coulomb = jnp.dot(own, other.T, precision=lax.Precision.HIGHEST, preferred_element_type=jnp.float32)
    denom = e_own + e_other - eps_vir[:, None] - eps_vir[None, :]
    amps = coulomb / denom
    spin = 2.0 * amps - amps.T
    grad = jnp.dot(spin, other, precision=lax.Precision.HIGHEST, preferred_element_type=jnp.float32)
    dens = jnp.dot(amps, spin.T, precision=lax.Precision.HIGHEST, preferred_element_type=jnp.float32)
    return grad, dens


def reference(slabs, eps_occ, eps_vir):
    def step(carry, index):
        own = slabs[index]
        grad = jnp.zeros((V, NAUX), jnp.float32)
        dens = carry
        for mask in (1, 2, 3):
            partner = jnp.bitwise_xor(index, jnp.int32(mask)).astype(jnp.int32)
            other = slabs[partner]
            g_part, d_part = pair_terms(own, other, eps_occ[index], eps_occ[partner], eps_vir)
            grad = grad + g_part
            dens = dens + d_part
        return dens, grad

    start = jnp.zeros((V, V), jnp.float32)
    dens, grads = lax.scan(step, start, jnp.arange(NOCC, dtype=jnp.int32))
    return grads, dens / NOCC
```

```python
import functools

import jax
import jax.numpy as jnp
from jax import lax
from jax.experimental import pallas as pl
from jax.experimental.pallas import tpu as pltpu
from jax.sharding import PartitionSpec as P

MESH = pl.DeviceIdType.MESH
F32, BF16 = jnp.float32, jnp.bfloat16
CHUNKS = 4


def nt(a, b):
    return lax.dot_general(a, b, (((1,), (1,)), ((), ())), preferred_element_type=F32)


def nn(a, b):
    return lax.dot_general(a, b, (((1,), (0,)), ((), ())), preferred_element_type=F32)


def split(value):
    high = value.astype(BF16)
    return high, (value - high.astype(F32)).astype(BF16)


def product(dot, a, b):
    return dot(a[0], b[0]) + (dot(a[0], b[1]) + dot(a[1], b[0]))


def kernel(
    fused, n_grp, n_orb,
    eps_ref, vir_ref, slab_ref, grad_ref, dens_ref,
    own_hi, own_lo, own, xs, xs_hi, xs_lo, zs, zs_hi, zs_lo, ds, ds_hi, ds_lo,
    level, energy, part, from_grp, summed, from_orb, final, rows_out,
    own_sem, x_sem, z_sem, fx_sem, fz_sem, e_sem, g_sem, o_sem, h_sem,
):
    virt, naux = own.shape
    width = naux // CHUNKS
    half = CHUNKS // 2
    grp, orb = lax.axis_index("grp"), lax.axis_index("orb")
    x_id = orb + 1 - 2 * lax.rem(orb, 2)
    z_id = orb + 2 - 4 * lax.rem(orb // 2, 2)
    d_id = x_id + z_id - orb

    load = pltpu.make_async_copy(slab_ref, own, own_sem)
    load.start()

    barrier = pltpu.get_barrier_semaphore()
    greeted = 0
    if fused:
        for r in range(1, n_grp):
            pl.semaphore_signal(
                barrier, inc=1, device_id={"grp": lax.rem(grp + r, n_grp)}, device_id_type=MESH
            )
        for r in range(1, n_orb):
            pl.semaphore_signal(
                barrier, inc=1, device_id={"orb": lax.rem(orb + r, n_orb)}, device_id_type=MESH
            )
        greeted = n_grp + n_orb - 2
    else:
        for to in (x_id, z_id, d_id):
            pl.semaphore_signal(barrier, inc=1, device_id={"orb": to}, device_id_type=MESH)
        greeted = 3
    energy[3] = jnp.full(energy.shape[1:], eps_ref[0], F32)
    pl.semaphore_wait(barrier, greeted)

    def remote(src, dst, sems, slot, **to):
        return pltpu.make_async_remote_copy(
            src_ref=src, dst_ref=dst, send_sem=sems.at[0, slot], recv_sem=sems.at[1, slot],
            device_id=to, device_id_type=MESH,
        )

    def cols(c):
        return (slice(None), pl.ds(c * width, width))

    x_copy = [remote(slab_ref.at[cols(c)], xs.at[cols(c)], x_sem, c, orb=x_id) for c in range(CHUNKS)]
    z_copy = [remote(slab_ref.at[cols(c)], zs.at[cols(c)], z_sem, c, orb=z_id) for c in range(CHUNKS)]
    fx_copy = [remote(zs.at[cols(c)], ds.at[cols(c)], fx_sem, c, orb=x_id) for c in range(half)]
    fz_copy = [
        remote(xs.at[cols(c + half)], ds.at[cols(c + half)], fz_sem, c, orb=z_id) for c in range(half)
    ]
    e_copy = [
        remote(energy.at[3], energy.at[s], e_sem, s, orb=to) for s, to in enumerate((x_id, z_id, d_id))
    ]
    for copy in e_copy:
        copy.start()
    for s in range(CHUNKS):
        x_copy[(s + half) % CHUNKS].start()
        z_copy[s].start()

    row = jnp.broadcast_to(vir_ref[...][None, :], (virt, virt))
    level[...] = row + row.T
    load.wait()
    own_hi[...], own_lo[...] = split(own[...])

    def ref_pair(hi, lo, c):
        return hi[cols(c)], lo[cols(c)]

    def take(src, hi, lo, c):
        hi[cols(c)], lo[cols(c)] = split(src[cols(c)])

    def coulomb(a, b, c):
        return product(nt, ref_pair(*a, c), ref_pair(*b, c))

    mine, firsts, seconds, thirds = (own_hi, own_lo), (xs_hi, xs_lo), (zs_hi, zs_lo), (ds_hi, ds_lo)
    k_x = k_z = jnp.zeros((virt, virt), F32)
    for s in range(CHUNKS):
        c = (s + half) % CHUNKS
        x_copy[c].wait_recv()
        take(xs, *firsts, c)
        z_copy[s].wait_recv()
        take(zs, *seconds, s)
        if s == CHUNKS - 2:
            for f in range(half):
                fx_copy[f].start()
                fz_copy[f].start()
        k_x = k_x + coulomb(mine, firsts, c)
        k_z = k_z + coulomb(mine, seconds, s)
    k_xz = jnp.zeros((virt, virt), F32)
    for c in range(CHUNKS):
        k_xz = k_xz + coulomb(firsts, seconds, c)
    for copy in e_copy:
        copy.wait_recv()
    e_x, e_z, e_d, e_own = (energy[s][:1, :1] for s in range(4))

    def amplitudes(k, energies):
        amps = k / (energies - level[...])
        return amps, 2.0 * amps - amps.T

    t_x, s_x = amplitudes(k_x, e_own + e_x)
    t_z, s_z = amplitudes(k_z, e_own + e_z)
    t_xz, s_xz = amplitudes(k_xz, e_x + e_z)
    s_x, s_z = split(s_x), split(s_z)
    density = (
        product(nt, split(t_x), s_x)
        + product(nt, split(t_z), s_z)
        + product(nt, split(t_xz), split(s_xz))
    )

    def gradient(spin, src, c):
        return product(nn, spin, ref_pair(*src, c))

    waits = []
    if fused:
        part[...] = density.reshape(part.shape)
        g_copy = [
            remote(part.at[:, lax.rem(grp + r, n_grp)], from_grp.at[r - 1], g_sem, r - 1,
                   grp=lax.rem(grp + r, n_grp))
            for r in range(1, n_grp)
        ]
        for copy in g_copy:
            copy.start()
    else:
        dens_ref[...] = density

    for c in range(CHUNKS):
        grad_ref[cols(c)] = gradient(s_x, firsts, c)

    if fused:
        for copy in g_copy:
            copy.wait_recv()
        total = part[:, pl.ds(grp, 1)][:, 0]
        for r in range(n_grp - 1):
            total = total + from_grp[r]
        summed[...] = total
        o_copy = [
            remote(summed.at[lax.rem(orb + r, n_orb)], from_orb.at[r - 1], o_sem, r - 1,
                   orb=lax.rem(orb + r, n_orb))
            for r in range(1, n_orb)
        ]
        for copy in o_copy:
            copy.start()
        waits += g_copy + o_copy

    for c in range(CHUNKS):
        grad_ref[cols(c)] += gradient(s_z, seconds, c)

    if fused:
        for copy in o_copy:
            copy.wait_recv()
        total = summed[pl.ds(orb, 1)][0]
        for r in range(n_orb - 1):
            total = total + from_orb[r]
        final[...] = total * (1.0 / (n_grp * n_orb))
        h_copy = [
            remote(final, rows_out.at[r - 1], h_sem, r - 1, grp=lax.rem(grp + r, n_grp))
            for r in range(1, n_grp)
        ]
        for copy in h_copy:
            copy.start()
        waits += h_copy

    k_d = jnp.zeros((virt, virt), F32)
    for f in range(half):
        for copy, c in ((fx_copy[f], f), (fz_copy[f], f + half)):
            copy.wait_recv()
            take(ds, *thirds, c)
            k_d = k_d + coulomb(mine, thirds, c)
    _, s_d = amplitudes(k_d, e_own + e_d)
    s_d = split(s_d)
    for c in range(CHUNKS):
        grad_ref[cols(c)] += gradient(s_d, thirds, c)

    if fused:
        block = final.shape[0]
        dens_ref[pl.ds(pl.multiple_of(grp * block, block), block), :] = final[...]
        for r in range(1, n_grp):
            h_copy[r - 1].wait_recv()
            at = lax.rem(grp + (n_grp - r), n_grp)
            dens_ref[pl.ds(pl.multiple_of(at * block, block), block), :] = rows_out[r - 1]
    for copy in x_copy + z_copy + fx_copy + fz_copy + e_copy + waits:
        copy.wait_send()


def per_device(slabs, eps_occ, eps_vir):
    own = slabs[0]
    virt, naux = own.shape
    n_grp, n_orb = lax.axis_size("grp"), lax.axis_size("orb")
    rows = virt // n_orb
    block = rows // n_grp
    fused = rows % n_grp == 0 and block % 8 == 0
    if not fused:
        block = 8
    whole = (virt, naux)
    wide = [pltpu.VMEM(whole, BF16)] * 2
    dma = lambda count: pltpu.SemaphoreType.DMA((2, count))
    gradient, density = pl.pallas_call(
        functools.partial(kernel, fused, n_grp, n_orb),
        out_shape=(
            jax.ShapeDtypeStruct(whole, F32),
            jax.ShapeDtypeStruct((rows if fused else virt, virt), F32),
        ),
        in_specs=[
            pl.BlockSpec(memory_space=pltpu.SMEM),
            pl.BlockSpec(memory_space=pltpu.VMEM),
            pl.BlockSpec(memory_space=pl.ANY),
        ],
        out_specs=(pl.BlockSpec(memory_space=pltpu.VMEM),) * 2,
        scratch_shapes=[
            *wide,
            pltpu.VMEM(whole, F32),
            *([pltpu.VMEM(whole, F32), *wide] * 3),
            pltpu.VMEM((virt, virt), F32),
            pltpu.VMEM((4, 8, 128), F32),
            pltpu.VMEM((n_orb, n_grp, block, virt), F32),
            pltpu.VMEM((n_grp - 1, n_orb, block, virt), F32),
            pltpu.VMEM((n_orb, block, virt), F32),
            pltpu.VMEM((n_orb - 1, block, virt), F32),
            pltpu.VMEM((block, virt), F32),
            pltpu.VMEM((n_grp - 1, block, virt), F32),
            pltpu.SemaphoreType.DMA,
            dma(CHUNKS), dma(CHUNKS), dma(CHUNKS // 2), dma(CHUNKS // 2), dma(3),
            dma(n_grp - 1), dma(n_orb - 1), dma(n_grp - 1),
        ],
        compiler_params=pltpu.CompilerParams(
            collective_id=0, has_side_effects=True, vmem_limit_bytes=40 * 2**20
        ),
        cost_estimate=pl.CostEstimate(
            flops=18 * virt * virt * (2 * naux + virt), bytes_accessed=8 * virt * naux, transcendentals=0
        ),
    )(eps_occ, eps_vir, own)
    if not fused:
        share = lax.psum_scatter(density, "orb", scatter_dimension=0, tiled=True)
        density = lax.psum(share, "grp") / (n_grp * n_orb)
    return gradient[None], density


def solution(mesh):
    placed = (P(("grp", "orb"), None, None), P(("grp", "orb")), P())
    return jax.shard_map(
        per_device,
        mesh=mesh,
        in_specs=placed,
        out_specs=(P(("grp", "orb"), None, None), P("orb", None)),
        check_vma=False,
    )
```
